32 devices in a mesh: dp: 16 (over z, x, core), tensor: 2 (over y).
Axes of the slice: x: 2, y: 2, z: 4, core: 2. Of those that a mesh axis runs over, the one named last changes fastest.
Arguments:
- latent_pre: bfloat16 [8192, 512], P('dp'), may hold values from -6 to 6
- norm_gain: float32 [512], replicated, may hold values from 0.1 to 1.9
- kv_weight: bfloat16 [512, 4096], P(None, 'tensor'), may hold values from -0.25 to 0.25
- down_weight: bfloat16 [7168, 512], P('tensor'), may hold values from -0.25 to 0.25
- grad_kv: bfloat16 [8192, 4096], P('dp', 'tensor'), may hold values from -0.75 to 0.75
- master: float32 [512, 4096], P('dp', 'tensor'), may hold values from -0.25 to 0.25
- first_moment: float32 [512, 4096], P('dp', 'tensor'), may hold values from -120 to 120
- second_moment: float32 [512, 4096], P('dp', 'tensor'), may hold values from 100 to 1000
Outputs:
- grad_hidden: bfloat16 [8192, 7168], P('dp', 'tensor')
- new_master: float32 [512, 4096], P('dp', 'tensor')
- new_first: float32 [512, 4096], P('dp', 'tensor')
- new_second: float32 [512, 4096], P('dp', 'tensor')
- new_replica: bfloat16 [512, 4096], P(None, 'tensor')
The draws below stay inside these ranges and needn't reach their ends.
All inputs are finite; a program needn't handle non-finite values.
Results may differ from the reference program's by a relative error of at most 0.002.
The reference program's roundings to bfloat16 on the way (of `normalized` and `grad_pre`) count: a program that leaves them out, or rounds other values in their place, can miss the bound.
Values may be sent and summed in bfloat16 or wider, within the bound.
A program may use at most 64 MiB of HBM per device.

```python
import math
import jax
import jax.numpy as jnp
from jax import lax

D = 7168
LATENT = 512
KV_COLS = 4096
TOKENS = 8192


def raised(array, key, source, target, shards_of, factor):
    owner, partner = [(jnp.arange(array.shape[axis_at]) // (array.shape[axis_at] // shards_of)).reshape([-1 if axis == axis_at else 1 for axis in range(array.ndim)]) for axis_at in (source, target)]
    chosen = jax.random.permutation(key, shards_of)[partner]
    strong = (owner == chosen) | (owner == (partner + shards_of // 2) % shards_of)
    return jnp.where(strong, factor * array, array)


def shard_levels(stream_key, dims, shards, least, largest):
    def one(axis_at, parts):
        heights = jax.random.uniform(jax.random.fold_in(jax.random.fold_in(stream_key, 6), axis_at), (parts,), jnp.float32, least / len(shards), largest / len(shards))
        return jnp.repeat(jnp.exp(heights), dims[axis_at] // parts).reshape((-1,) + (1,) * (len(dims) - axis_at - 1))

    gain = one(*shards[0])
    for cut in shards[1:]:
        gain = gain * one(*cut)
    return gain


def bell_draw(own_key, shape, width, bound, cuts=(), kind=jnp.bfloat16):
    array = width * jax.random.normal(own_key, shape, jnp.float32)
    if cuts:
        array = array * shard_levels(own_key, shape, cuts, -0.22, 0.18)
    return jnp.clip(array, -bound, bound).astype(kind)


def heavy_noise(key, dims, deviation, most, cuts, heavy, held_as=jnp.bfloat16):
    values = deviation * jax.random.normal(key, dims, jnp.float32)
    if cuts:
        values = values * shard_levels(key, dims, cuts, -0.22, 0.18)
    return jnp.clip(raised(values, jax.random.fold_in(key, 3), *heavy), -most, most).astype(held_as)


def setup_inputs(seed: int = 0) -> dict:
    key_of = jax.random.split(jax.random.key(seed), 9)
    return {
        "latent_pre": heavy_noise(key_of[0], (TOKENS, LATENT), 1.0, 6.0, ((0, 16),), (0, 1, 16, 2.0)),
        "norm_gain": jnp.clip(1.0 + 0.18 * jax.random.normal(key_of[1], (LATENT,), jnp.float32), 0.1, 1.9),
        "kv_weight": bell_draw(key_of[2], (LATENT, KV_COLS), LATENT ** -0.5, 0.25, ((1, 2),)),
        "down_weight": bell_draw(key_of[3], (D, LATENT), LATENT ** -0.5, 0.25, ((0, 2),)),
        "grad_kv": bell_draw(key_of[4], (TOKENS, KV_COLS), 0.125, 0.75, ((0, 16), (1, 2))),
        "master": bell_draw(key_of[5], (LATENT, KV_COLS), LATENT ** -0.5, 0.25, ((0, 16), (1, 2)), jnp.float32),
        "first_moment": bell_draw(key_of[6], (LATENT, KV_COLS), 20.0, 120.0, ((0, 16), (1, 2)), jnp.float32),
        "second_moment": jnp.clip(jnp.exp(math.log(1000.0) - 2.3025851 * jax.random.uniform(key_of[7], (LATENT, KV_COLS), jnp.float32) ** shard_levels(key_of[7], (LATENT, KV_COLS), ((0, 16), (1, 2)), -0.2, 0.2)), 100.0, 1000.0),
    }


bias_first = 0.9999734386011124
bias_second = 0.09520785288629112

def reference(latent_pre, norm_gain, kv_weight, down_weight, grad_kv, master, first_moment, second_moment):
    values = latent_pre.astype(jnp.float32)
    inverse_rms = lax.rsqrt(lax.optimization_barrier(jnp.mean(values * values, axis=1, keepdims=True)) + 1e-06)
    unit = values * inverse_rms
    normalized = (unit * norm_gain).astype(jnp.bfloat16)
    grad_latent = lax.dot_general(grad_kv, kv_weight, (((1,), (1,)), ((), ())), preferred_element_type=jnp.float32)
    scaled = grad_latent * norm_gain
    inner = lax.optimization_barrier(jnp.mean(scaled * unit, axis=1, keepdims=True))
    grad_pre = (inverse_rms * (scaled - unit * inner)).astype(jnp.bfloat16)
    grad_hidden = lax.dot_general(grad_pre, down_weight, (((1,), (1,)), ((), ())), preferred_element_type=jnp.float32).astype(jnp.bfloat16)
    weight_grad = lax.dot_general(normalized, grad_kv, (((0,), (0,)), ((), ())), preferred_element_type=jnp.float32)
    new_first = 0.9 * first_moment + 0.1 * weight_grad
    new_second = 0.999 * second_moment + 0.001 * weight_grad * weight_grad
    first_hat = new_first / bias_first
    second_hat = new_second / bias_second
    new_master = master - 0.01 * (first_hat / (jnp.sqrt(second_hat) + 1e-08) + 0.1 * master)
    return (grad_hidden, new_master, new_first, new_second, new_master.astype(jnp.bfloat16))
```

```python
import functools

import jax
import jax.numpy as jnp
from jax import lax
from jax.experimental import pallas as pl
from jax.experimental.pallas import tpu as pltpu
from jax.sharding import PartitionSpec as P

bias_first = 0.9999734386011124
bias_second = 0.09520785288629112
MESH = pl.DeviceIdType.MESH


def norm_backward(latent_rows, norm_gain, grad_rows):
    values = latent_rows.astype(jnp.float32)
    inverse_rms = lax.rsqrt(jnp.mean(values * values, axis=1, keepdims=True) + 1e-06)
    unit = values * inverse_rms
    scaled = grad_rows * norm_gain
    inner = jnp.mean(scaled * unit, axis=1, keepdims=True)
    return (inverse_rms * (scaled - unit * inner)).astype(jnp.bfloat16)


def normalize(latent_pre, norm_gain):
    values = latent_pre.astype(jnp.float32)
    inverse_rms = lax.rsqrt(jnp.mean(values * values, axis=1, keepdims=True) + 1e-06)
    return values * inverse_rms * norm_gain


def adamw(master, first_moment, second_moment, weight_grad):
    new_first = 0.9 * first_moment + 0.1 * weight_grad
    new_second = 0.999 * second_moment + 0.001 * weight_grad * weight_grad
    first_hat = new_first / bias_first
    second_hat = new_second / bias_second
    new_master = master - 0.01 * (first_hat / (jnp.sqrt(second_hat) + 1e-08) + 0.1 * master)
    return new_master, new_first, new_second


def project(grad_pre, down_weight):
    return lax.dot_general(
        grad_pre, down_weight, (((1,), (1,)), ((), ())), preferred_element_type=jnp.float32
    ).astype(jnp.bfloat16)


def local_small_rows(
    latent_pre, norm_gain, kv_weight, down_weight, grad_kv, master, first_moment, second_moment
):
    normalized = normalize(latent_pre, norm_gain).astype(jnp.bfloat16)
    partial_grad = lax.dot_general(
        grad_kv, kv_weight, (((1,), (1,)), ((), ())), preferred_element_type=jnp.float32
    )
    grad_latent = lax.psum(partial_grad, "tensor")
    grad_hidden = project(norm_backward(latent_pre, norm_gain, grad_latent), down_weight)
    weight_grad = lax.psum_scatter(
        lax.dot_general(
            normalized, grad_kv, (((0,), (0,)), ((), ())), preferred_element_type=jnp.float32
        ),
        "dp",
        scatter_dimension=0,
        tiled=True,
    )
    new_master, new_first, new_second = adamw(master, first_moment, second_moment, weight_grad)
    new_replica = lax.all_gather(new_master.astype(jnp.bfloat16), "dp", axis=0, tiled=True)
    return (grad_hidden, new_master, new_first, new_second, new_replica)


def kernel(
    Z, T, K,
    latent, gain, kvw, gkv, master, first, second,
    gp, new_master, new_first, new_second, rep,
    norm_t, acc, core_in, x_out, x_in, z_out, z_in, lat_out, lat_in, lat_own,
    core_s, core_r, x_s, x_r, z_s, z_r, lat_s, lat_r, gp_s, gp_r,
    agz_s, agz_r, agx_s, agx_r, agc_s, agc_r,
):
    me = lax.axis_index("dp")
    t = lax.axis_index("tensor")
    z, x, c = me // 4, (me // 2) % 2, me % 2
    rows, W = acc.shape[-2], acc.shape[-1]
    half = lat_own.shape[0]

    def at(zz, xx, cc):
        return zz * 4 + xx * 2 + cc

    core_peer = {"dp": at(z, x, 1 - c)}
    x_peer = {"dp": at(z, 1 - x, c)}
    z_to = [None] + [lax.rem(z + d, Z) for d in range(1, Z)]
    z_from = [z] + [lax.rem(z - d + Z, Z) for d in range(1, Z)]
    t_to = [None] + [lax.rem(t + d, T) for d in range(1, T)]

    barrier = pltpu.get_barrier_semaphore()
    peers = [core_peer, x_peer]
    peers += [{"dp": at(z_to[d], x, c)} for d in range(1, Z)]
    peers += [{"tensor": t_to[d]} for d in range(1, T)]
    for peer in peers:
        pl.semaphore_signal(barrier, inc=1, device_id=peer, device_id_type=MESH)

    started = []

    def send(src, dst, s, r, peer):
        copy = pltpu.make_async_remote_copy(
            src_ref=src, dst_ref=dst, send_sem=s, recv_sem=r, device_id=peer, device_id_type=MESH
        )
        copy.start()
        started.append(copy)
        return copy

    norm_t[...] = jnp.transpose(normalize(latent[...], gain[...])).astype(jnp.bfloat16)

    def weight_chunk(k):
        part = jnp.dot(
            norm_t[...], gkv[:, k * W:(k + 1) * W], preferred_element_type=jnp.float32
        )
        acc[k] = part.reshape(Z, 2, 2, rows, W)

    def send_core(k):
        return send(
            acc.at[k, :, :, 1 - c], core_in.at[k], core_s.at[k], core_r.at[k], core_peer
        )

    def latent_part(index):
        start = pl.multiple_of(index * half, half)
        return lax.dot_general(
            gkv[pl.ds(start, half), :], kvw[...], (((1,), (1,)), ((), ())),
            preferred_element_type=jnp.float32,
        )

    weight_chunk(0)
    pl.semaphore_wait(barrier, len(peers))
    core = [send_core(0)]
    lat = [None]
    for d in range(1, T):
        lat_out[d - 1] = latent_part(t_to[d])
        lat.append(send(
            lat_out.at[d - 1], lat_in.at[d - 1], lat_s.at[d - 1], lat_r.at[d - 1],
            {"tensor": t_to[d]},
        ))
    xs = []

    def stage_x(k):
        core[k].wait_recv()
        x_out[k] = (acc[k, :, 1 - x, c] + core_in[k, :, 1 - x]).astype(jnp.bfloat16)
        xs.append(send(x_out.at[k], x_in.at[k], x_s.at[k], x_r.at[k], x_peer))

    for k in range(1, K):
        weight_chunk(k)
        core.append(send_core(k))
        stage_x(k - 1)
    stage_x(K - 1)
    lat_own[...] = latent_part(t)

    def block_sum(k, zz):
        return acc[k, zz, x, c] + core_in[k, zz, x] + x_in[k, zz].astype(jnp.float32)

    zs = []
    for k in range(K):
        xs[k].wait_recv()
        zs.append([])
        for d in range(1, Z):
            z_out[k, d - 1] = block_sum(k, z_to[d]).astype(jnp.bfloat16)
            zs[k].append(send(
                z_out.at[k, d - 1], z_in.at[k, d - 1], z_s.at[k, d - 1], z_r.at[k, d - 1],
                {"dp": at(z_to[d], x, c)},
            ))

    def gather(zz, xx, cc, k, s, r, peer):
        block = rep.at[at(zz, xx, cc), :, pl.ds(k * W, W)]
        return send(block, block, s, r, peer)

    agz, agx, agc = [], [], []

    def update(k):
        for copy in zs[k]:
            copy.wait_recv()
        total = block_sum(k, z)
        for d in range(1, Z):
            total = total + z_in[k, d - 1].astype(jnp.float32)
        cols = slice(k * W, (k + 1) * W)
        fresh, new_first[:, cols], new_second[:, cols] = adamw(
            master[:, cols], first[:, cols], second[:, cols], total
        )
        new_master[:, cols] = fresh
        rep[me, :, cols] = fresh.astype(jnp.bfloat16)
        agz.append([
            gather(z, x, c, k, agz_s.at[k, d - 1], agz_r.at[k, d - 1], {"dp": at(z_to[d], x, c)})
            for d in range(1, Z)
        ])
        agx.append([gather(z, x, c, k, agx_s.at[k, 0], agx_r.at[k, 0], x_peer)])
        agc.append([gather(z, x, c, k, agc_s.at[k, 0], agc_r.at[k, 0], core_peer)])

    def forward(k):
        for d in range(1, Z):
            agz[k][d - 1].wait_recv()
            agx[k].append(
                gather(z_from[d], x, c, k, agx_s.at[k, d], agx_r.at[k, d], x_peer)
            )
            agc[k].append(
                gather(z_from[d], x, c, k, agc_s.at[k, d], agc_r.at[k, d], core_peer)
            )

    def forward_core(k):
        for d in range(Z):
            agx[k][d].wait_recv()
            agc[k].append(gather(
                z_from[d], 1 - x, c, k, agc_s.at[k, Z + d], agc_r.at[k, Z + d], core_peer
            ))

    update(0)
    grad = lat_own[...]
    for d in range(1, T):
        lat[d].wait_recv()
        grad = grad + lat_in[d - 1]
    gp[t] = norm_backward(latent[pl.ds(pl.multiple_of(t * half, half), half), :], gain[...], grad)
    gps = [
        send(gp.at[t], gp.at[t], gp_s.at[d - 1], gp_r.at[d - 1], {"tensor": t_to[d]})
        for d in range(1, T)
    ]
    for k in range(1, K):
        update(k)
        forward(k - 1)
        if k >= 2:
            forward_core(k - 2)
    forward(K - 1)
    for k in range(max(K - 2, 0), K):
        forward_core(k)
    for k in range(K):
        for copy in agc[k]:
            copy.wait_recv()
    for copy in gps:
        copy.wait_recv()
    for copy in started:
        copy.wait_send()


def local(
    Z, T,
    latent_pre, norm_gain, kv_weight, down_weight, grad_kv, master, first_moment, second_moment,
):
    tokens, width = latent_pre.shape
    rows, columns = master.shape
    dp, half, K = 4 * Z, tokens // T, 4
    W = columns // K
    f32, bf16, DMA = jnp.float32, jnp.bfloat16, pltpu.SemaphoreType.DMA
    state = jax.ShapeDtypeStruct((rows, columns), f32)
    vmem = pl.BlockSpec(memory_space=pltpu.VMEM)
    grad_pre, new_master, new_first, new_second, replica = pl.pallas_call(
        functools.partial(kernel, Z, T, K),
        out_shape=(
            jax.ShapeDtypeStruct((T, half, width), bf16),
            state, state, state,
            jax.ShapeDtypeStruct((dp, rows, columns), bf16),
        ),
        in_specs=[vmem] * 7,
        out_specs=(vmem,) * 5,
        scratch_shapes=[
            pltpu.VMEM((width, tokens), bf16),
            pltpu.VMEM((K, Z, 2, 2, rows, W), f32),
            pltpu.VMEM((K, Z, 2, rows, W), f32),
            pltpu.VMEM((K, Z, rows, W), bf16),
            pltpu.VMEM((K, Z, rows, W), bf16),
            pltpu.VMEM((K, Z - 1, rows, W), bf16),
            pltpu.VMEM((K, Z - 1, rows, W), bf16),
            pltpu.VMEM((T - 1, half, width), f32),
            pltpu.VMEM((T - 1, half, width), f32),
            pltpu.VMEM((half, width), f32),
            DMA((K,)), DMA((K,)), DMA((K,)), DMA((K,)),
            DMA((K, Z - 1)), DMA((K, Z - 1)),
            DMA((T - 1,)), DMA((T - 1,)), DMA((T - 1,)), DMA((T - 1,)),
            DMA((K, Z - 1)), DMA((K, Z - 1)),
            DMA((K, Z)), DMA((K, Z)),
            DMA((K, 2 * Z)), DMA((K, 2 * Z)),
        ],
        compiler_params=pltpu.CompilerParams(
            collective_id=0, has_side_effects=True, vmem_limit_bytes=40 * 1024 * 1024
        ),
    )(latent_pre, norm_gain.reshape(1, width), kv_weight, grad_kv, master, first_moment, second_moment)
    grad_hidden = project(grad_pre.reshape(tokens, width), down_weight)
    return (grad_hidden, new_master, new_first, new_second, replica.reshape(dp * rows, columns))


def solution(mesh):
    dp, T = mesh.shape["dp"], mesh.shape["tensor"]

    def body(*args):
        rows = args[5].shape[0]
        if dp % 4 == 0 and dp > 4 and T > 1 and rows % 16 == 0:
            return local(dp // 4, T, *args)
        return local_small_rows(*args)

    placed = (
        P("dp", None),
        P(),
        P(None, "tensor"),
        P("tensor", None),
        P("dp", "tensor"),
        P("dp", "tensor"),
        P("dp", "tensor"),
        P("dp", "tensor"),
    )
    return jax.shard_map(
        body,
        mesh=mesh,
        in_specs=placed,
        out_specs=(
            P("dp", "tensor"),
            P("dp", "tensor"),
            P("dp", "tensor"),
            P("dp", "tensor"),
            P(None, "tensor"),
        ),
        check_vma=False,
    )
```

```python
import functools

import jax
import jax.numpy as jnp
from jax import lax
from jax.experimental import pallas as pl
from jax.experimental.pallas import tpu as pltpu
from jax.sharding import PartitionSpec as P

bias_first = 0.9999734386011124
bias_second = 0.09520785288629112
MESH = pl.DeviceIdType.MESH


def norm_backward(latent_rows, norm_gain, grad_rows):
    values = latent_rows.astype(jnp.float32)
    inverse_rms = lax.rsqrt(jnp.mean(values * values, axis=1, keepdims=True) + 1e-06)
    unit = values * inverse_rms
    scaled = grad_rows * norm_gain
    inner = jnp.mean(scaled * unit, axis=1, keepdims=True)
    return (inverse_rms * (scaled - unit * inner)).astype(jnp.bfloat16)


def normalize(latent_pre, norm_gain):
    values = latent_pre.astype(jnp.float32)
    inverse_rms = lax.rsqrt(jnp.mean(values * values, axis=1, keepdims=True) + 1e-06)
    return values * inverse_rms * norm_gain


def adamw(master, first_moment, second_moment, weight_grad):
    new_first = 0.9 * first_moment + 0.1 * weight_grad
    new_second = 0.999 * second_moment + 0.001 * weight_grad * weight_grad
    first_hat = new_first / bias_first
    second_hat = new_second / bias_second
    new_master = master - 0.01 * (first_hat / (jnp.sqrt(second_hat) + 1e-08) + 0.1 * master)
    return new_master, new_first, new_second


def project(grad_pre, down_weight):
    return lax.dot_general(
        grad_pre, down_weight, (((1,), (1,)), ((), ())), preferred_element_type=jnp.float32
    ).astype(jnp.bfloat16)


def local_small_rows(
    latent_pre, norm_gain, kv_weight, down_weight, grad_kv, master, first_moment, second_moment
):
    normalized = normalize(latent_pre, norm_gain).astype(jnp.bfloat16)
    partial_grad = lax.dot_general(
        grad_kv, kv_weight, (((1,), (1,)), ((), ())), preferred_element_type=jnp.float32
    )
    grad_latent = lax.psum(partial_grad, "tensor")
    grad_hidden = project(norm_backward(latent_pre, norm_gain, grad_latent), down_weight)
    weight_grad = lax.psum_scatter(
        lax.dot_general(
            normalized, grad_kv, (((0,), (0,)), ((), ())), preferred_element_type=jnp.float32
        ),
        "dp",
        scatter_dimension=0,
        tiled=True,
    )
    new_master, new_first, new_second = adamw(master, first_moment, second_moment, weight_grad)
    new_replica = lax.all_gather(new_master.astype(jnp.bfloat16), "dp", axis=0, tiled=True)
    return (grad_hidden, new_master, new_first, new_second, new_replica)


def kernel(
    Z, T, K,
    latent_h, gain_h, kvw_h, gkv_h, master_h, first_h, second_h,
    gp, new_master, new_first, new_second, rep,
    latent, gain, kvw, gkv, master, first, second, load_s, gkv_s,
    norm_t, acc, core_in, x_out, x_in, z_out, z_in, lat_out, lat_in, lat_own,
    core_s, core_r, x_s, x_r, z_s, z_r, lat_s, lat_r, gp_s, gp_r,
    agz_s, agz_r, agx_s, agx_r, agc_s, agc_r,
):
    rows, W = acc.shape[-2], acc.shape[-1]
    pairs = (
        (latent_h, latent), (gain_h, gain), (kvw_h, kvw),
        (master_h, master), (first_h, first), (second_h, second),
    )
    loads = [pltpu.make_async_copy(a, b, load_s.at[i]) for i, (a, b) in enumerate(pairs)]
    gkv_loads = [
        pltpu.make_async_copy(
            gkv_h.at[:, pl.ds(k * W, W)], gkv.at[:, pl.ds(k * W, W)], gkv_s.at[k]
        )
        for k in range(K)
    ]
    for copy in loads[:2] + gkv_loads + loads[2:]:
        copy.start()

    me = lax.axis_index("dp")
    t = lax.axis_index("tensor")
    z, x, c = me // 4, (me // 2) % 2, me % 2
    half = lat_own.shape[0]

    def at(zz, xx, cc):
        return zz * 4 + xx * 2 + cc

    core_peer = {"dp": at(z, x, 1 - c)}
    x_peer = {"dp": at(z, 1 - x, c)}
    z_to = [None] + [lax.rem(z + d, Z) for d in range(1, Z)]
    z_from = [z] + [lax.rem(z - d + Z, Z) for d in range(1, Z)]
    t_to = [None] + [lax.rem(t + d, T) for d in range(1, T)]

    barrier = pltpu.get_barrier_semaphore()
    peers = [core_peer, x_peer]
    peers += [{"dp": at(z_to[d], x, c)} for d in range(1, Z)]
    peers += [{"tensor": t_to[d]} for d in range(1, T)]
    for peer in peers:
        pl.semaphore_signal(barrier, inc=1, device_id=peer, device_id_type=MESH)

    started = []

    def send(src, dst, s, r, peer):
        copy = pltpu.make_async_remote_copy(
            src_ref=src, dst_ref=dst, send_sem=s, recv_sem=r, device_id=peer, device_id_type=MESH
        )
        copy.start()
        started.append(copy)
        return copy

    loads[0].wait()
    loads[1].wait()
    norm_t[...] = jnp.transpose(normalize(latent[...], gain[...])).astype(jnp.bfloat16)

    def weight_chunk(k):
        part = jnp.dot(
            norm_t[...], gkv[:, k * W:(k + 1) * W], preferred_element_type=jnp.float32
        )
        acc[k] = part.reshape(Z, 2, 2, rows, W)

    def send_core(k):
        return send(
            acc.at[k, :, :, 1 - c], core_in.at[k], core_s.at[k], core_r.at[k], core_peer
        )

    def latent_part(index):
        start = pl.multiple_of(index * half, half)
        return lax.dot_general(
            gkv[pl.ds(start, half), :], kvw[...], (((1,), (1,)), ((), ())),
            preferred_element_type=jnp.float32,
        )

    gkv_loads[0].wait()
    weight_chunk(0)
    pl.semaphore_wait(barrier, len(peers))
    core = [send_core(0)]
    for copy in gkv_loads[1:]:
        copy.wait()
    loads[2].wait()
    lat = [None]
    for d in range(1, T):
        lat_out[d - 1] = latent_part(t_to[d])
        lat.append(send(
            lat_out.at[d - 1], lat_in.at[d - 1], lat_s.at[d - 1], lat_r.at[d - 1],
            {"tensor": t_to[d]},
        ))
    xs = []

    def stage_x(k):
        core[k].wait_recv()
        x_out[k] = (acc[k, :, 1 - x, c] + core_in[k, :, 1 - x]).astype(jnp.bfloat16)
        xs.append(send(x_out.at[k], x_in.at[k], x_s.at[k], x_r.at[k], x_peer))

    for k in range(1, K):
        weight_chunk(k)
        core.append(send_core(k))
        stage_x(k - 1)
    stage_x(K - 1)
    lat_own[...] = latent_part(t)

    def block_sum(k, zz):
        return acc[k, zz, x, c] + core_in[k, zz, x] + x_in[k, zz].astype(jnp.float32)

    zs = []
    for k in range(K):
        xs[k].wait_recv()
        zs.append([])
        for d in range(1, Z):
            z_out[k, d - 1] = block_sum(k, z_to[d]).astype(jnp.bfloat16)
            zs[k].append(send(
                z_out.at[k, d - 1], z_in.at[k, d - 1], z_s.at[k, d - 1], z_r.at[k, d - 1],
                {"dp": at(z_to[d], x, c)},
            ))

    def gather(zz, xx, cc, k, s, r, peer):
        block = rep.at[at(zz, xx, cc), :, pl.ds(k * W, W)]
        return send(block, block, s, r, peer)

    agz, agx, agc = [], [], []

    def update(k):
        for copy in zs[k]:
            copy.wait_recv()
        total = block_sum(k, z)
        for d in range(1, Z):
            total = total + z_in[k, d - 1].astype(jnp.float32)
        cols = slice(k * W, (k + 1) * W)
        fresh, new_first[:, cols], new_second[:, cols] = adamw(
            master[:, cols], first[:, cols], second[:, cols], total
        )
        new_master[:, cols] = fresh
        rep[me, :, cols] = fresh.astype(jnp.bfloat16)
        agz.append([
            gather(z, x, c, k, agz_s.at[k, d - 1], agz_r.at[k, d - 1], {"dp": at(z_to[d], x, c)})
            for d in range(1, Z)
        ])
        agx.append([gather(z, x, c, k, agx_s.at[k, 0], agx_r.at[k, 0], x_peer)])
        agc.append([gather(z, x, c, k, agc_s.at[k, 0], agc_r.at[k, 0], core_peer)])

    def forward(k):
        for d in range(1, Z):
            agz[k][d - 1].wait_recv()
            agx[k].append(
                gather(z_from[d], x, c, k, agx_s.at[k, d], agx_r.at[k, d], x_peer)
            )
            agc[k].append(
                gather(z_from[d], x, c, k, agc_s.at[k, d], agc_r.at[k, d], core_peer)
            )

    def forward_core(k):
        for d in range(Z):
            agx[k][d].wait_recv()
            agc[k].append(gather(
                z_from[d], 1 - x, c, k, agc_s.at[k, Z + d], agc_r.at[k, Z + d], core_peer
            ))

    for copy in loads[3:]:
        copy.wait()
    update(0)
    grad = lat_own[...]
    for d in range(1, T):
        lat[d].wait_recv()
        grad = grad + lat_in[d - 1]
    gp[t] = norm_backward(latent[pl.ds(pl.multiple_of(t * half, half), half), :], gain[...], grad)
    gps = [
        send(gp.at[t], gp.at[t], gp_s.at[d - 1], gp_r.at[d - 1], {"tensor": t_to[d]})
        for d in range(1, T)
    ]
    for k in range(1, K):
        update(k)
        forward(k - 1)
        if k >= 2:
            forward_core(k - 2)
    forward(K - 1)
    for k in range(max(K - 2, 0), K):
        forward_core(k)
    for k in range(K):
        for copy in agc[k]:
            copy.wait_recv()
    for copy in gps:
        copy.wait_recv()
    for copy in started:
        copy.wait_send()


def finish(
    gp_h, down_h, master, first, second, rep,
    hidden_h, master_h, first_h, second_h, rep_h,
    gp, gp_s, down, down_s, tiles, out_s, tile_s,
):
    count, _, tile = tiles.shape
    load = pltpu.make_async_copy(gp_h, gp, gp_s)
    load.start()
    down_loads = [
        pltpu.make_async_copy(down_h.at[pl.ds(n * tile, tile), :], down.at[n], down_s.at[n])
        for n in range(count)
    ]
    for copy in down_loads:
        copy.start()
    pairs = ((rep, rep_h), (master, master_h), (first, first_h), (second, second_h))
    copies = [pltpu.make_async_copy(a, b, out_s.at[i]) for i, (a, b) in enumerate(pairs)]
    for copy in copies:
        copy.start()
    load.wait()
    for n in range(count):
        down_loads[n].wait()
        tiles[n] = project(gp[...], down[n])
        copies.append(pltpu.make_async_copy(
            tiles.at[n], hidden_h.at[:, pl.ds(n * tile, tile)], tile_s.at[n]
        ))
        copies[-1].start()
    for copy in copies:
        copy.wait()


def local(
    Z, T,
    latent_pre, norm_gain, kv_weight, down_weight, grad_kv, master, first_moment, second_moment,
):
    tokens, width = latent_pre.shape
    rows, columns = master.shape
    dp, half, K = 4 * Z, tokens // T, 4
    W = columns // K
    f32, bf16, DMA = jnp.float32, jnp.bfloat16, pltpu.SemaphoreType.DMA
    state = jax.ShapeDtypeStruct((rows, columns), f32)
    vmem = pl.BlockSpec(memory_space=pltpu.VMEM)
    grad_pre, new_master, new_first, new_second, replica = pl.pallas_call(
        functools.partial(kernel, Z, T, K),
        out_shape=(
            jax.ShapeDtypeStruct((T, half, width), bf16),
            state, state, state,
            jax.ShapeDtypeStruct((dp, rows, columns), bf16),
        ),
        in_specs=[pl.BlockSpec(memory_space=pltpu.HBM)] * 7,
        out_specs=(vmem,) * 5,
        scratch_shapes=[
            pltpu.VMEM((tokens, width), bf16),
            pltpu.VMEM((1, width), f32),
            pltpu.VMEM((width, columns), bf16),
            pltpu.VMEM((tokens, columns), bf16),
            pltpu.VMEM((rows, columns), f32),
            pltpu.VMEM((rows, columns), f32),
            pltpu.VMEM((rows, columns), f32),
            DMA((6,)), DMA((K,)),
            pltpu.VMEM((width, tokens), bf16),
            pltpu.VMEM((K, Z, 2, 2, rows, W), f32),
            pltpu.VMEM((K, Z, 2, rows, W), f32),
            pltpu.VMEM((K, Z, rows, W), bf16),
            pltpu.VMEM((K, Z, rows, W), bf16),
            pltpu.VMEM((K, Z - 1, rows, W), bf16),
            pltpu.VMEM((K, Z - 1, rows, W), bf16),
            pltpu.VMEM((T - 1, half, width), f32),
            pltpu.VMEM((T - 1, half, width), f32),
            pltpu.VMEM((half, width), f32),
            DMA((K,)), DMA((K,)), DMA((K,)), DMA((K,)),
            DMA((K, Z - 1)), DMA((K, Z - 1)),
            DMA((T - 1,)), DMA((T - 1,)), DMA((T - 1,)), DMA((T - 1,)),
            DMA((K, Z - 1)), DMA((K, Z - 1)),
            DMA((K, Z)), DMA((K, Z)),
            DMA((K, 2 * Z)), DMA((K, 2 * Z)),
        ],
        compiler_params=pltpu.CompilerParams(
            collective_id=0, has_side_effects=True, vmem_limit_bytes=58 * 1024 * 1024
        ),
    )(latent_pre, norm_gain.reshape(1, width), kv_weight, grad_kv, master, first_moment, second_moment)
    model = down_weight.shape[0]
    tile = next(n for n in (512, 256, 128, model) if model % n == 0)
    any_space = pl.BlockSpec(memory_space=pltpu.HBM)
    return pl.pallas_call(
        finish,
        out_shape=(
            jax.ShapeDtypeStruct((tokens, model), bf16),
            state, state, state,
            jax.ShapeDtypeStruct((dp * rows, columns), bf16),
        ),
        in_specs=[any_space] * 6,
        out_specs=(any_space,) * 5,
        scratch_shapes=[
            pltpu.VMEM((tokens, width), bf16), DMA,
            pltpu.VMEM((model // tile, tile, width), bf16), DMA((model // tile,)),
            pltpu.VMEM((model // tile, tokens, tile), bf16),
            DMA((4,)), DMA((model // tile,)),
        ],
        compiler_params=pltpu.CompilerParams(vmem_limit_bytes=60 * 1024 * 1024),
    )(
        grad_pre.reshape(tokens, width), down_weight, new_master, new_first, new_second,
        replica.reshape(dp * rows, columns),
    )


def solution(mesh):
    dp, T = mesh.shape["dp"], mesh.shape["tensor"]

    def body(*args):
        rows = args[5].shape[0]
        if dp % 4 == 0 and dp > 4 and T > 1 and rows % 16 == 0:
            return local(dp // 4, T, *args)
        return local_small_rows(*args)

    placed = (
        P("dp", None),
        P(),
        P(None, "tensor"),
        P("tensor", None),
        P("dp", "tensor"),
        P("dp", "tensor"),
        P("dp", "tensor"),
        P("dp", "tensor"),
    )
    return jax.shard_map(
        body,
        mesh=mesh,
        in_specs=placed,
        out_specs=(
            P("dp", "tensor"),
            P("dp", "tensor"),
            P("dp", "tensor"),
            P("dp", "tensor"),
            P(None, "tensor"),
        ),
        check_vma=False,
    )
```

```python
import functools

import jax
import jax.numpy as jnp
from jax import lax
from jax.experimental import pallas as pl
from jax.experimental.pallas import tpu as pltpu
from jax.sharding import PartitionSpec as P

bias_first = 0.9999734386011124
bias_second = 0.09520785288629112
MESH = pl.DeviceIdType.MESH


def norm_backward(latent_rows, norm_gain, grad_rows):
    values = latent_rows.astype(jnp.float32)
    inverse_rms = lax.rsqrt(jnp.mean(values * values, axis=1, keepdims=True) + 1e-06)
    unit = values * inverse_rms
    scaled = grad_rows * norm_gain
    inner = jnp.mean(scaled * unit, axis=1, keepdims=True)
    return (inverse_rms * (scaled - unit * inner)).astype(jnp.bfloat16)


def normalize(latent_pre, norm_gain):
    values = latent_pre.astype(jnp.float32)
    inverse_rms = lax.rsqrt(jnp.mean(values * values, axis=1, keepdims=True) + 1e-06)
    return values * inverse_rms * norm_gain


def adamw(master, first_moment, second_moment, weight_grad):
    new_first = 0.9 * first_moment + 0.1 * weight_grad
    new_second = 0.999 * second_moment + 0.001 * weight_grad * weight_grad
    first_hat = new_first / bias_first
    second_hat = new_second / bias_second
    new_master = master - 0.01 * (first_hat / (jnp.sqrt(second_hat) + 1e-08) + 0.1 * master)
    return new_master, new_first, new_second


def project(grad_pre, down_weight):
    return lax.dot_general(
        grad_pre, down_weight, (((1,), (1,)), ((), ())), preferred_element_type=jnp.float32
    ).astype(jnp.bfloat16)


def local_small_rows(
    latent_pre, norm_gain, kv_weight, down_weight, grad_kv, master, first_moment, second_moment
):
    normalized = normalize(latent_pre, norm_gain).astype(jnp.bfloat16)
    partial_grad = lax.dot_general(
        grad_kv, kv_weight, (((1,), (1,)), ((), ())), preferred_element_type=jnp.float32
    )
    grad_latent = lax.psum(partial_grad, "tensor")
    grad_hidden = project(norm_backward(latent_pre, norm_gain, grad_latent), down_weight)
    weight_grad = lax.psum_scatter(
        lax.dot_general(
            normalized, grad_kv, (((0,), (0,)), ((), ())), preferred_element_type=jnp.float32
        ),
        "dp",
        scatter_dimension=0,
        tiled=True,
    )
    new_master, new_first, new_second = adamw(master, first_moment, second_moment, weight_grad)
    new_replica = lax.all_gather(new_master.astype(jnp.bfloat16), "dp", axis=0, tiled=True)
    return (grad_hidden, new_master, new_first, new_second, new_replica)


def kernel(
    Z, T, K,
    latent_h, gain_h, kvw_h, gkv_h, master_h, first_h, second_h,
    gp, new_master, new_first, new_second, rep,
    latent, gain, kvw, gkv, master, first, second, load_s, gkv_s,
    norm_t, acc, core_in, x_out, x_in, z_out, z_in, lat_out, lat_in, lat_own,
    core_s, core_r, x_s, x_r, z_s, z_r, lat_s, lat_r, gp_s, gp_r,
    agz_s, agz_r, agx_s, agx_r, agc_s, agc_r,
):
    rows, W = acc.shape[-2], acc.shape[-1]
    pairs = (
        (latent_h, latent), (gain_h, gain), (kvw_h, kvw),
        (master_h, master), (first_h, first), (second_h, second),
    )
    loads = [pltpu.make_async_copy(a, b, load_s.at[i]) for i, (a, b) in enumerate(pairs)]
    gkv_loads = [
        pltpu.make_async_copy(
            gkv_h.at[:, pl.ds(k * W, W)], gkv.at[:, pl.ds(k * W, W)], gkv_s.at[k]
        )
        for k in range(K)
    ]
    for copy in loads[:2] + gkv_loads + loads[2:]:
        copy.start()

    me = lax.axis_index("dp")
    t = lax.axis_index("tensor")
    z, x, c = me // 4, (me // 2) % 2, me % 2
    half = lat_own.shape[0]

    def at(zz, xx, cc):
        return zz * 4 + xx * 2 + cc

    core_peer = {"dp": at(z, x, 1 - c)}
    x_peer = {"dp": at(z, 1 - x, c)}
    z_to = [None] + [lax.rem(z + d, Z) for d in range(1, Z)]
    z_from = [z] + [lax.rem(z - d + Z, Z) for d in range(1, Z)]
    t_to = [None] + [lax.rem(t + d, T) for d in range(1, T)]

    barrier = pltpu.get_barrier_semaphore()
    peers = [core_peer, x_peer]
    peers += [{"dp": at(z_to[d], x, c)} for d in range(1, Z)]
    peers += [{"tensor": t_to[d]} for d in range(1, T)]
    for peer in peers:
        pl.semaphore_signal(barrier, inc=1, device_id=peer, device_id_type=MESH)

    started = []

    def send(src, dst, s, r, peer):
        copy = pltpu.make_async_remote_copy(
            src_ref=src, dst_ref=dst, send_sem=s, recv_sem=r, device_id=peer, device_id_type=MESH
        )
        copy.start()
        started.append(copy)
        return copy

    loads[0].wait()
    loads[1].wait()
    norm_t[...] = jnp.transpose(normalize(latent[...], gain[...])).astype(jnp.bfloat16)

    def weight_chunk(k):
        part = jnp.dot(
            norm_t[...], gkv[:, k * W:(k + 1) * W], preferred_element_type=jnp.float32
        )
        acc[k] = part.reshape(Z, 2, 2, rows, W)

    def send_core(k):
        return send(
            acc.at[k, :, :, 1 - c], core_in.at[k], core_s.at[k], core_r.at[k], core_peer
        )

    def latent_part(index):
        start = pl.multiple_of(index * half, half)
        return lax.dot_general(
            gkv[pl.ds(start, half), :], kvw[...], (((1,), (1,)), ((), ())),
            preferred_element_type=jnp.float32,
        )

    gkv_loads[0].wait()
    weight_chunk(0)
    pl.semaphore_wait(barrier, len(peers))
    core = [send_core(0)]
    for copy in gkv_loads[1:]:
        copy.wait()
    loads[2].wait()
    lat = [None]
    for d in range(1, T):
        lat_out[d - 1] = latent_part(t_to[d])
        lat.append(send(
            lat_out.at[d - 1], lat_in.at[d - 1], lat_s.at[d - 1], lat_r.at[d - 1],
            {"tensor": t_to[d]},
        ))
    xs = []

    def stage_x(k):
        core[k].wait_recv()
        x_out[k] = (acc[k, :, 1 - x, c] + core_in[k, :, 1 - x]).astype(jnp.bfloat16)
        xs.append(send(x_out.at[k], x_in.at[k], x_s.at[k], x_r.at[k], x_peer))

    for k in range(1, K):
        weight_chunk(k)
        core.append(send_core(k))
        stage_x(k - 1)
    stage_x(K - 1)
    lat_own[...] = latent_part(t)

    def block_sum(k, zz):
        return acc[k, zz, x, c] + core_in[k, zz, x] + x_in[k, zz].astype(jnp.float32)

    zs = []
    for k in range(K):
        xs[k].wait_recv()
        zs.append([])
        for d in range(1, Z):
            z_out[k, d - 1] = block_sum(k, z_to[d]).astype(jnp.bfloat16)
            zs[k].append(send(
                z_out.at[k, d - 1], z_in.at[k, d - 1], z_s.at[k, d - 1], z_r.at[k, d - 1],
                {"dp": at(z_to[d], x, c)},
            ))

    def gather(zz, xx, cc, k, s, r, peer):
        block = rep.at[at(zz, xx, cc), :, pl.ds(k * W, W)]
        return send(block, block, s, r, peer)

    agz, agx, agc = [], [], []

    def update(k):
        for copy in zs[k]:
            copy.wait_recv()
        total = block_sum(k, z)
        for d in range(1, Z):
            total = total + z_in[k, d - 1].astype(jnp.float32)
        cols = slice(k * W, (k + 1) * W)
        fresh, new_first[:, cols], new_second[:, cols] = adamw(
            master[:, cols], first[:, cols], second[:, cols], total
        )
        new_master[:, cols] = fresh
        rep[me, :, cols] = fresh.astype(jnp.bfloat16)
        agz.append([
            gather(z, x, c, k, agz_s.at[k, d - 1], agz_r.at[k, d - 1], {"dp": at(z_to[d], x, c)})
            for d in range(1, Z)
        ])
        agx.append([gather(z, x, c, k, agx_s.at[k, 0], agx_r.at[k, 0], x_peer)])
        agc.append([gather(z, x, c, k, agc_s.at[k, 0], agc_r.at[k, 0], core_peer)])

    def forward(k):
        for d in range(1, Z):
            agz[k][d - 1].wait_recv()
            agx[k].append(
                gather(z_from[d], x, c, k, agx_s.at[k, d], agx_r.at[k, d], x_peer)
            )
            agc[k].append(
                gather(z_from[d], x, c, k, agc_s.at[k, d], agc_r.at[k, d], core_peer)
            )

    def forward_core(k):
        for d in range(Z):
            agx[k][d].wait_recv()
            agc[k].append(gather(
                z_from[d], 1 - x, c, k, agc_s.at[k, Z + d], agc_r.at[k, Z + d], core_peer
            ))

    for copy in loads[3:]:
        copy.wait()
    update(0)
    grad = lat_own[...]
    for d in range(1, T):
        lat[d].wait_recv()
        grad = grad + lat_in[d - 1]
    gp[t] = norm_backward(latent[pl.ds(pl.multiple_of(t * half, half), half), :], gain[...], grad)
    gps = [
        send(gp.at[t], gp.at[t], gp_s.at[d - 1], gp_r.at[d - 1], {"tensor": t_to[d]})
        for d in range(1, T)
    ]
    for k in range(1, K):
        update(k)
        forward(k - 1)
        if k >= 2:
            forward_core(k - 2)
    forward(K - 1)
    for k in range(max(K - 2, 0), K):
        forward_core(k)
    for k in range(K):
        for copy in agc[k]:
            copy.wait_recv()
    for copy in gps:
        copy.wait_recv()
    for copy in started:
        copy.wait_send()


def finish(
    gp_h, down_h, master, first, second, rep,
    hidden_h, master_h, first_h, second_h, rep_h,
    gp, gp_s, down, down_s, tiles, out_s, tile_s,
    rep_v, master_v, first_v, second_v, in_s,
):
    count, _, tile = tiles.shape
    load = pltpu.make_async_copy(gp_h, gp, gp_s)
    load.start()
    down_loads = [
        pltpu.make_async_copy(down_h.at[pl.ds(n * tile, tile), :], down.at[n], down_s.at[n])
        for n in range(count)
    ]
    for copy in down_loads:
        copy.start()
    trips = (
        (rep, rep_v, rep_h), (master, master_v, master_h),
        (first, first_v, first_h), (second, second_v, second_h),
    )
    arrivals = [pltpu.make_async_copy(a, v, in_s.at[i]) for i, (a, v, _) in enumerate(trips)]
    for copy in arrivals:
        copy.start()
    copies = []
    load.wait()
    for n in range(count):
        down_loads[n].wait()
        tiles[n] = project(gp[...], down[n])
        copies.append(pltpu.make_async_copy(
            tiles.at[n], hidden_h.at[:, pl.ds(n * tile, tile)], tile_s.at[n]
        ))
        copies[-1].start()
        if n == 0:
            for i, (_, v, b) in enumerate(trips):
                arrivals[i].wait()
                copies.append(pltpu.make_async_copy(v, b, out_s.at[i]))
                copies[-1].start()
    for copy in copies:
        copy.wait()


def local(
    Z, T,
    latent_pre, norm_gain, kv_weight, down_weight, grad_kv, master, first_moment, second_moment,
):
    tokens, width = latent_pre.shape
    rows, columns = master.shape
    dp, half, K = 4 * Z, tokens // T, 4
    W = columns // K
    f32, bf16, DMA = jnp.float32, jnp.bfloat16, pltpu.SemaphoreType.DMA
    state = jax.ShapeDtypeStruct((rows, columns), f32)
    vmem = pl.BlockSpec(memory_space=pltpu.VMEM)
    grad_pre, new_master, new_first, new_second, replica = pl.pallas_call(
        functools.partial(kernel, Z, T, K),
        out_shape=(
            jax.ShapeDtypeStruct((T, half, width), bf16),
            state, state, state,
            jax.ShapeDtypeStruct((dp, rows, columns), bf16),
        ),
        in_specs=[pl.BlockSpec(memory_space=pltpu.HBM)] * 7,
        out_specs=(vmem,) * 5,
        scratch_shapes=[
            pltpu.VMEM((tokens, width), bf16),
            pltpu.VMEM((1, width), f32),
            pltpu.VMEM((width, columns), bf16),
            pltpu.VMEM((tokens, columns), bf16),
            pltpu.VMEM((rows, columns), f32),
            pltpu.VMEM((rows, columns), f32),
            pltpu.VMEM((rows, columns), f32),
            DMA((6,)), DMA((K,)),
            pltpu.VMEM((width, tokens), bf16),
            pltpu.VMEM((K, Z, 2, 2, rows, W), f32),
            pltpu.VMEM((K, Z, 2, rows, W), f32),
            pltpu.VMEM((K, Z, rows, W), bf16),
            pltpu.VMEM((K, Z, rows, W), bf16),
            pltpu.VMEM((K, Z - 1, rows, W), bf16),
            pltpu.VMEM((K, Z - 1, rows, W), bf16),
            pltpu.VMEM((T - 1, half, width), f32),
            pltpu.VMEM((T - 1, half, width), f32),
            pltpu.VMEM((half, width), f32),
            DMA((K,)), DMA((K,)), DMA((K,)), DMA((K,)),
            DMA((K, Z - 1)), DMA((K, Z - 1)),
            DMA((T - 1,)), DMA((T - 1,)), DMA((T - 1,)), DMA((T - 1,)),
            DMA((K, Z - 1)), DMA((K, Z - 1)),
            DMA((K, Z)), DMA((K, Z)),
            DMA((K, 2 * Z)), DMA((K, 2 * Z)),
        ],
        compiler_params=pltpu.CompilerParams(
            collective_id=0, has_side_effects=True, vmem_limit_bytes=58 * 1024 * 1024
        ),
    )(latent_pre, norm_gain.reshape(1, width), kv_weight, grad_kv, master, first_moment, second_moment)
    model = down_weight.shape[0]
    tile = next(n for n in (512, 256, 128, model) if model % n == 0)
    any_space = pl.BlockSpec(memory_space=pltpu.HBM)
    return pl.pallas_call(
        finish,
        out_shape=(
            jax.ShapeDtypeStruct((tokens, model), bf16),
            state, state, state,
            jax.ShapeDtypeStruct((dp * rows, columns), bf16),
        ),
        in_specs=[any_space] * 6,
        out_specs=(any_space,) * 5,
        scratch_shapes=[
            pltpu.VMEM((tokens, width), bf16), DMA,
            pltpu.VMEM((model // tile, tile, width), bf16), DMA((model // tile,)),
            pltpu.VMEM((model // tile, tokens, tile), bf16),
            DMA((4,)), DMA((model // tile,)),
            pltpu.VMEM((dp * rows, columns), bf16),
            pltpu.VMEM((rows, columns), f32),
            pltpu.VMEM((rows, columns), f32),
            pltpu.VMEM((rows, columns), f32),
            DMA((4,)),
        ],
        compiler_params=pltpu.CompilerParams(vmem_limit_bytes=60 * 1024 * 1024),
    )(
        grad_pre.reshape(tokens, width), down_weight, new_master, new_first, new_second,
        replica.reshape(dp * rows, columns),
    )


def solution(mesh):
    dp, T = mesh.shape["dp"], mesh.shape["tensor"]

    def body(*args):
        rows = args[5].shape[0]
        if dp % 4 == 0 and dp > 4 and T > 1 and rows % 16 == 0:
            return local(dp // 4, T, *args)
        return local_small_rows(*args)

    placed = (
        P("dp", None),
        P(),
        P(None, "tensor"),
        P("tensor", None),
        P("dp", "tensor"),
        P("dp", "tensor"),
        P("dp", "tensor"),
        P("dp", "tensor"),
    )
    return jax.shard_map(
        body,
        mesh=mesh,
        in_specs=placed,
        out_specs=(
            P("dp", "tensor"),
            P("dp", "tensor"),
            P("dp", "tensor"),
            P("dp", "tensor"),
            P(None, "tensor"),
        ),
        check_vma=False,
    )
```

```python
import functools

import jax
import jax.numpy as jnp
from jax import lax
from jax.experimental import pallas as pl
from jax.experimental.pallas import tpu as pltpu
from jax.sharding import PartitionSpec as P

bias_first = 0.9999734386011124
bias_second = 0.09520785288629112
MESH = pl.DeviceIdType.MESH


def norm_backward(latent_rows, norm_gain, grad_rows):
    values = latent_rows.astype(jnp.float32)
    inverse_rms = lax.rsqrt(jnp.mean(values * values, axis=1, keepdims=True) + 1e-06)
    unit = values * inverse_rms
    scaled = grad_rows * norm_gain
    inner = jnp.mean(scaled * unit, axis=1, keepdims=True)
    return (inverse_rms * (scaled - unit * inner)).astype(jnp.bfloat16)


def normalize(latent_pre, norm_gain):
    values = latent_pre.astype(jnp.float32)
    inverse_rms = lax.rsqrt(jnp.mean(values * values, axis=1, keepdims=True) + 1e-06)
    return values * inverse_rms * norm_gain


def adamw(master, first_moment, second_moment, weight_grad):
    new_first = 0.9 * first_moment + 0.1 * weight_grad
    new_second = 0.999 * second_moment + 0.001 * weight_grad * weight_grad
    first_hat = new_first / bias_first
    second_hat = new_second / bias_second
    new_master = master - 0.01 * (first_hat / (jnp.sqrt(second_hat) + 1e-08) + 0.1 * master)
    return new_master, new_first, new_second


def project(grad_pre, down_weight):
    return lax.dot_general(
        grad_pre, down_weight, (((1,), (1,)), ((), ())), preferred_element_type=jnp.float32
    ).astype(jnp.bfloat16)


def local_small_rows(
    latent_pre, norm_gain, kv_weight, down_weight, grad_kv, master, first_moment, second_moment
):
    normalized = normalize(latent_pre, norm_gain).astype(jnp.bfloat16)
    partial_grad = lax.dot_general(
        grad_kv, kv_weight, (((1,), (1,)), ((), ())), preferred_element_type=jnp.float32
    )
    grad_latent = lax.psum(partial_grad, "tensor")
    grad_hidden = project(norm_backward(latent_pre, norm_gain, grad_latent), down_weight)
    weight_grad = lax.psum_scatter(
        lax.dot_general(
            normalized, grad_kv, (((0,), (0,)), ((), ())), preferred_element_type=jnp.float32
        ),
        "dp",
        scatter_dimension=0,
        tiled=True,
    )
    new_master, new_first, new_second = adamw(master, first_moment, second_moment, weight_grad)
    new_replica = lax.all_gather(new_master.astype(jnp.bfloat16), "dp", axis=0, tiled=True)
    return (grad_hidden, new_master, new_first, new_second, new_replica)


def kernel(
    Z, T, K,
    latent_h, gain_h, kvw_h, gkv_h, master_h, first_h, second_h,
    gp, new_master, new_first, new_second, rep,
    latent, gain, kvw, gkv, master, first, second, load_s, gkv_s,
    norm_t, acc, core_in, x_out, x_in, z_out, z_in, lat_out, lat_in, lat_own,
    core_s, core_r, x_s, x_r, z_s, z_r, lat_s, lat_r, gp_s, gp_r,
    agz_s, agz_r, agx_s, agx_r, agc_s, agc_r,
):
    rows, W = acc.shape[-2], acc.shape[-1]
    pairs = (
        (latent_h, latent), (gain_h, gain), (kvw_h, kvw),
        (master_h, master), (first_h, first), (second_h, second),
    )
    loads = [pltpu.make_async_copy(a, b, load_s.at[i]) for i, (a, b) in enumerate(pairs)]
    gkv_loads = [
        pltpu.make_async_copy(
            gkv_h.at[:, pl.ds(k * W, W)], gkv.at[:, pl.ds(k * W, W)], gkv_s.at[k]
        )
        for k in range(K)
    ]
    for copy in loads[:2] + gkv_loads + loads[2:]:
        copy.start()

    me = lax.axis_index("dp")
    t = lax.axis_index("tensor")
    z, x, c = me // 4, (me // 2) % 2, me % 2
    half = lat_own.shape[0]

    def at(zz, xx, cc):
        return zz * 4 + xx * 2 + cc

    core_peer = {"dp": at(z, x, 1 - c)}
    x_peer = {"dp": at(z, 1 - x, c)}
    z_to = [None] + [lax.rem(z + d, Z) for d in range(1, Z)]
    z_from = [z] + [lax.rem(z - d + Z, Z) for d in range(1, Z)]
    t_to = [None] + [lax.rem(t + d, T) for d in range(1, T)]

    barrier = pltpu.get_barrier_semaphore()
    peers = [core_peer, x_peer]
    peers += [{"dp": at(z_to[d], x, c)} for d in range(1, Z)]
    peers += [{"tensor": t_to[d]} for d in range(1, T)]
    for peer in peers:
        pl.semaphore_signal(barrier, inc=1, device_id=peer, device_id_type=MESH)

    started = []

    def send(src, dst, s, r, peer):
        copy = pltpu.make_async_remote_copy(
            src_ref=src, dst_ref=dst, send_sem=s, recv_sem=r, device_id=peer, device_id_type=MESH
        )
        copy.start()
        started.append(copy)
        return copy

    loads[0].wait()
    loads[1].wait()
    norm_t[...] = jnp.transpose(normalize(latent[...], gain[...])).astype(jnp.bfloat16)

    def weight_chunk(k):
        part = jnp.dot(
            norm_t[...], gkv[:, k * W:(k + 1) * W], preferred_element_type=jnp.float32
        )
        acc[k] = part.reshape(Z, 2, 2, rows, W)

    def send_core(k):
        return send(
            acc.at[k, :, :, 1 - c], core_in.at[k], core_s.at[k], core_r.at[k], core_peer
        )

    def latent_part(index):
        start = pl.multiple_of(index * half, half)
        return lax.dot_general(
            gkv[pl.ds(start, half), :], kvw[...], (((1,), (1,)), ((), ())),
            preferred_element_type=jnp.float32,
        )

    gkv_loads[0].wait()
    weight_chunk(0)
    pl.semaphore_wait(barrier, len(peers))
    core = [send_core(0)]
    for copy in gkv_loads[1:]:
        copy.wait()
    loads[2].wait()
    lat = [None]
    for d in range(1, T):
        lat_out[d - 1] = latent_part(t_to[d])
        lat.append(send(
            lat_out.at[d - 1], lat_in.at[d - 1], lat_s.at[d - 1], lat_r.at[d - 1],
            {"tensor": t_to[d]},
        ))
    xs = []

    def stage_x(k):
        core[k].wait_recv()
        x_out[k] = (acc[k, :, 1 - x, c] + core_in[k, :, 1 - x]).astype(jnp.bfloat16)
        xs.append(send(x_out.at[k], x_in.at[k], x_s.at[k], x_r.at[k], x_peer))

    for k in range(1, K):
        weight_chunk(k)
        core.append(send_core(k))
        stage_x(k - 1)
    stage_x(K - 1)
    lat_own[...] = latent_part(t)

    def block_sum(k, zz):
        return acc[k, zz, x, c] + core_in[k, zz, x] + x_in[k, zz].astype(jnp.float32)

    zs = []
    for k in range(K):
        xs[k].wait_recv()
        zs.append([])
        for d in range(1, Z):
            z_out[k, d - 1] = block_sum(k, z_to[d]).astype(jnp.bfloat16)
            zs[k].append(send(
                z_out.at[k, d - 1], z_in.at[k, d - 1], z_s.at[k, d - 1], z_r.at[k, d - 1],
                {"dp": at(z_to[d], x, c)},
            ))

    def gather(zz, xx, cc, k, s, r, peer):
        block = rep.at[k, zz, xx, cc]
        return send(block, block, s, r, peer)

    agz, agx, agc = [], [], []

    def update(k):
        for copy in zs[k]:
            copy.wait_recv()
        total = block_sum(k, z)
        for d in range(1, Z):
            total = total + z_in[k, d - 1].astype(jnp.float32)
        cols = slice(k * W, (k + 1) * W)
        fresh, new_first[:, cols], new_second[:, cols] = adamw(
            master[:, cols], first[:, cols], second[:, cols], total
        )
        new_master[:, cols] = fresh
        rep[k, z, x, c] = fresh.astype(jnp.bfloat16)
        agz.append([
            gather(z, x, c, k, agz_s.at[k, d - 1], agz_r.at[k, d - 1], {"dp": at(z_to[d], x, c)})
            for d in range(1, Z)
        ])
        agx.append([gather(z, x, c, k, agx_s.at[k, 0], agx_r.at[k, 0], x_peer)])
        agc.append([])

    def whole_core(k, xx, i):
        block = rep.at[k, :, xx, c]
        agc[k].append(send(block, block, agc_s.at[k, i], agc_r.at[k, i], core_peer))

    def forward(k):
        for d in range(1, Z):
            agz[k][d - 1].wait_recv()
            agx[k].append(
                gather(z_from[d], x, c, k, agx_s.at[k, d], agx_r.at[k, d], x_peer)
            )
        whole_core(k, x, 0)

    def forward_core(k):
        for d in range(Z):
            agx[k][d].wait_recv()
        whole_core(k, 1 - x, 1)

    for copy in loads[3:]:
        copy.wait()
    update(0)
    grad = lat_own[...]
    for d in range(1, T):
        lat[d].wait_recv()
        grad = grad + lat_in[d - 1]
    gp[t] = norm_backward(latent[pl.ds(pl.multiple_of(t * half, half), half), :], gain[...], grad)
    gps = [
        send(gp.at[t], gp.at[t], gp_s.at[d - 1], gp_r.at[d - 1], {"tensor": t_to[d]})
        for d in range(1, T)
    ]
    for k in range(1, K):
        update(k)
        forward(k - 1)
        if k >= 2:
            forward_core(k - 2)
    forward(K - 1)
    for k in range(max(K - 2, 0), K):
        forward_core(k)
    for k in range(K):
        for copy in agc[k]:
            copy.wait_recv()
    for copy in gps:
        copy.wait_recv()
    for copy in started:
        copy.wait_send()


def finish(
    gp_h, down_h, master, first, second, rep,
    hidden_h, master_h, first_h, second_h, rep_h,
    gp, gp_s, down, down_s, tiles, out_s, tile_s,
    rep_v, master_v, first_v, second_v, in_s,
):
    count, _, tile = tiles.shape
    load = pltpu.make_async_copy(gp_h, gp, gp_s)
    load.start()
    down_loads = [
        pltpu.make_async_copy(down_h.at[pl.ds(n * tile, tile), :], down.at[n], down_s.at[n])
        for n in range(count)
    ]
    for copy in down_loads:
        copy.start()
    trips = (
        (rep, rep_v, rep_h), (master, master_v, master_h),
        (first, first_v, first_h), (second, second_v, second_h),
    )
    arrivals = [
        pltpu.make_async_copy(a, v, in_s.at[i]) for i, (a, v, _) in enumerate(trips[1:])
    ]
    K, _, W = rep.shape
    arrivals += [
        pltpu.make_async_copy(rep.at[k], rep_v.at[:, pl.ds(k * W, W)], in_s.at[3 + k])
        for k in range(K)
    ]
    for copy in arrivals:
        copy.start()
    copies = []
    load.wait()
    for n in range(count):
        down_loads[n].wait()
        tiles[n] = project(gp[...], down[n])
        copies.append(pltpu.make_async_copy(
            tiles.at[n], hidden_h.at[:, pl.ds(n * tile, tile)], tile_s.at[n]
        ))
        copies[-1].start()
        if n == 0:
            for copy in arrivals:
                copy.wait()
            for i, (_, v, b) in enumerate(trips):
                copies.append(pltpu.make_async_copy(v, b, out_s.at[i]))
                copies[-1].start()
    for copy in copies:
        copy.wait()


def local(
    Z, T,
    latent_pre, norm_gain, kv_weight, down_weight, grad_kv, master, first_moment, second_moment,
):
    tokens, width = latent_pre.shape
    rows, columns = master.shape
    dp, half, K = 4 * Z, tokens // T, 4
    W = columns // K
    f32, bf16, DMA = jnp.float32, jnp.bfloat16, pltpu.SemaphoreType.DMA
    state = jax.ShapeDtypeStruct((rows, columns), f32)
    vmem = pl.BlockSpec(memory_space=pltpu.VMEM)
    grad_pre, new_master, new_first, new_second, replica = pl.pallas_call(
        functools.partial(kernel, Z, T, K),
        out_shape=(
            jax.ShapeDtypeStruct((T, half, width), bf16),
            state, state, state,
            jax.ShapeDtypeStruct((K, Z, 2, 2, rows, W), bf16),
        ),
        in_specs=[pl.BlockSpec(memory_space=pltpu.HBM)] * 7,
        out_specs=(vmem,) * 5,
        scratch_shapes=[
            pltpu.VMEM((tokens, width), bf16),
            pltpu.VMEM((1, width), f32),
            pltpu.VMEM((width, columns), bf16),
            pltpu.VMEM((tokens, columns), bf16),
            pltpu.VMEM((rows, columns), f32),
            pltpu.VMEM((rows, columns), f32),
            pltpu.VMEM((rows, columns), f32),
            DMA((6,)), DMA((K,)),
            pltpu.VMEM((width, tokens), bf16),
            pltpu.VMEM((K, Z, 2, 2, rows, W), f32),
            pltpu.VMEM((K, Z, 2, rows, W), f32),
            pltpu.VMEM((K, Z, rows, W), bf16),
            pltpu.VMEM((K, Z, rows, W), bf16),
            pltpu.VMEM((K, Z - 1, rows, W), bf16),
            pltpu.VMEM((K, Z - 1, rows, W), bf16),
            pltpu.VMEM((T - 1, half, width), f32),
            pltpu.VMEM((T - 1, half, width), f32),
            pltpu.VMEM((half, width), f32),
            DMA((K,)), DMA((K,)), DMA((K,)), DMA((K,)),
            DMA((K, Z - 1)), DMA((K, Z - 1)),
            DMA((T - 1,)), DMA((T - 1,)), DMA((T - 1,)), DMA((T - 1,)),
            DMA((K, Z - 1)), DMA((K, Z - 1)),
            DMA((K, Z)), DMA((K, Z)),
            DMA((K, 2)), DMA((K, 2)),
        ],
        compiler_params=pltpu.CompilerParams(
            collective_id=0, has_side_effects=True, vmem_limit_bytes=58 * 1024 * 1024
        ),
    )(latent_pre, norm_gain.reshape(1, width), kv_weight, grad_kv, master, first_moment, second_moment)
    model = down_weight.shape[0]
    tile = next(n for n in (512, 256, 128, model) if model % n == 0)
    any_space = pl.BlockSpec(memory_space=pltpu.HBM)
    return pl.pallas_call(
        finish,
        out_shape=(
            jax.ShapeDtypeStruct((tokens, model), bf16),
            state, state, state,
            jax.ShapeDtypeStruct((dp * rows, columns), bf16),
        ),
        in_specs=[any_space] * 6,
        out_specs=(any_space,) * 5,
        scratch_shapes=[
            pltpu.VMEM((tokens, width), bf16), DMA,
            pltpu.VMEM((model // tile, tile, width), bf16), DMA((model // tile,)),
            pltpu.VMEM((model // tile, tokens, tile), bf16),
            DMA((4,)), DMA((model // tile,)),
            pltpu.VMEM((dp * rows, columns), bf16),
            pltpu.VMEM((rows, columns), f32),
            pltpu.VMEM((rows, columns), f32),
            pltpu.VMEM((rows, columns), f32),
            DMA((3 + K,)),
        ],
        compiler_params=pltpu.CompilerParams(vmem_limit_bytes=60 * 1024 * 1024),
    )(
        grad_pre.reshape(tokens, width), down_weight, new_master, new_first, new_second,
        replica.reshape(K, dp * rows, W),
    )


def solution(mesh):
    dp, T = mesh.shape["dp"], mesh.shape["tensor"]

    def body(*args):
        rows = args[5].shape[0]
        if dp % 4 == 0 and dp > 4 and T > 1 and rows % 16 == 0:
            return local(dp // 4, T, *args)
        return local_small_rows(*args)

    placed = (
        P("dp", None),
        P(),
        P(None, "tensor"),
        P("tensor", None),
        P("dp", "tensor"),
        P("dp", "tensor"),
        P("dp", "tensor"),
        P("dp", "tensor"),
    )
    return jax.shard_map(
        body,
        mesh=mesh,
        in_specs=placed,
        out_specs=(
            P("dp", "tensor"),
            P("dp", "tensor"),
            P("dp", "tensor"),
            P("dp", "tensor"),
            P(None, "tensor"),
        ),
        check_vma=False,
    )
```
